256 devices in a mesh: row: 32 (over y, x, core), col: 8 (over z).
Axes of the slice: x: 4, y: 4, z: 8, core: 2. Of those that a mesh axis runs over, the one named last changes fastest.
Arguments:
- factor: float32 [2, 4096, 20, 4096], P(None, 'row', None, 'col'), as said below
- inverses: float32 [2, 4096, 4096], P(None, 'col', 'row'), as said below
- right_side: float32 [2, 4096, 64], P(None, 'row'), may hold values from -6 to 6
- earlier: float32 [18, 4096, 64], P(None, ('col', 'row')), may hold values from -6 to 6
Outputs:
- solved: float32 [2, 4096, 64], P(None, 'col')
The draws below stay inside these ranges and needn't reach their ends.
Inputs may be any that keep to these rules, and one draw needn't show every extreme that they name: factor[k] is zero in every block of centres numbered 18 + k or higher. Each inverses[k] is lower triangular with a positive diagonal.
All inputs are finite; a program needn't handle non-finite values.
Results may differ from the reference program's by a relative error of at most 0.0001.
Values sent between devices are 32-bit elements; how exact they have to be, the bound alone decides.
A program may use at most 128 MiB of HBM per device.

```python
import jax
import jax.numpy as jnp
from jax import lax

BLOCK = 4096
BLOCKS = 20
OUTS = 64
STEPS = 2
CENTRES = 81920
PRIOR = 18


def draw_factor(key, part):
    key = jax.random.fold_in(key, 11)
    first = jax.random.fold_in(key, 0)
    shape = (STEPS, BLOCK, BLOCKS, BLOCK)
    values = jax.random.normal(first, shape, jnp.float32) * CENTRES ** (-0.5)
    step_index = jnp.arange(STEPS)[:, None, None, None]
    block_index = jnp.arange(BLOCKS)[None, None, :, None]
    return jnp.where(block_index < PRIOR + step_index, values, 0.0).astype(jnp.float32)


def draw_inverses(key, part):
    key = jax.random.fold_in(key, 23)
    first, second = jax.random.split(key)
    shape = (STEPS, BLOCK, BLOCK)
    below = jax.random.normal(first, shape, jnp.float32) * (0.8 * BLOCK ** (-0.5))
    diagonal = jnp.exp(jax.random.uniform(second, (STEPS, BLOCK, 1), jnp.float32, -0.7, 0.7))
    row_index = jnp.arange(BLOCK)[None, :, None]
    col_index = jnp.arange(BLOCK)[None, None, :]
    values = jnp.where(col_index < row_index, below, 0.0)
    values = jnp.where(col_index == row_index, diagonal, values)
    return values.astype(jnp.float32)


def block_scale(rng, shape, cuts, low, high):
    factor_of = 1.0
    for axis_at, parts in cuts:
        steps = jax.random.uniform(jax.random.fold_in(jax.random.fold_in(rng, 6), axis_at), (parts,), jnp.float32, low / len(cuts), high / len(cuts))
        factor_of = factor_of * jnp.repeat(jnp.exp(steps), shape[axis_at] // parts).reshape((-1,) + (1,) * (len(shape) - 1 - axis_at))
    return factor_of


def bell_draw(key, dims, scale, bound, shards=(), kind=jnp.bfloat16):
    result = jax.random.normal(key, dims, jnp.float32) * scale
    if len(shards) > 0:
        result = block_scale(key, dims, shards, -0.22, 0.18) * result
    return jnp.clip(result, min=-bound, max=bound).astype(kind)


def setup_inputs(seed: int = 0) -> dict:
    seeds = jax.random.split(jax.random.key(seed), 5)
    return {
        "factor": draw_factor(jax.random.fold_in(seeds[4], 71), 0),
        "inverses": draw_inverses(jax.random.fold_in(seeds[4], 71), 0),
        "right_side": bell_draw(seeds[2], (STEPS, BLOCK, OUTS), 1.0, 6.0, ((1, 32),), jnp.float32),
        "earlier": bell_draw(seeds[3], (PRIOR, BLOCK, OUTS), 1.0, 6.0, ((1, 256),), jnp.float32),
    }


def reference(factor, inverses, right_side, earlier):
    known = earlier.reshape(PRIOR * BLOCK, OUTS)
    results = []
    for step in range(STEPS):
        width = known.shape[0]
        lower = factor[step].reshape(BLOCK, BLOCKS * BLOCK)[:, :width]
        total = jnp.dot(lower, known, precision=lax.Precision.HIGHEST, preferred_element_type=jnp.float32)
        value = jnp.dot(inverses[step], right_side[step] - total, precision=lax.Precision.HIGHEST, preferred_element_type=jnp.float32)
        results.append(value)
        known = jnp.concatenate([known, value], axis=0)
    return jnp.stack(results)
```

```python
import functools

import jax
import jax.numpy as jnp
from jax import lax
from jax.experimental import pallas as pl
from jax.experimental.pallas import tpu as pltpu
from jax.sharding import PartitionSpec as P

MESH = pl.DeviceIdType.MESH
F32 = jnp.float32
BF16 = jnp.bfloat16
CORES = 2


def split(value):
    high = value.astype(BF16)
    return high, (value - high.astype(F32)).astype(BF16)


def product(left, right):
    return jnp.dot(left, right, preferred_element_type=F32)


def kernel(
    side, planes, factor, inverses, right_side, earlier, solved,
    known, tiles, tiles_split, corner, inverse, inverse_split, corner_split, sums,
    mine, others, term, parts, pair, value,
    load_sem, send_sem, ring_sem, group_sem, core_sem, z_sem, scatter_sem, pair_sem, gather_sem,
):
    steps, prior, rows, width = tiles.shape
    half = prior // 2
    outs = right_side.shape[1]
    place = lax.axis_index("row")
    z = lax.axis_index("col")
    y, x, core = place // (side * CORES), (place // CORES) % side, place % CORES
    chips = side * side

    def chip_at(dy, dx):
        return (y + dy) % side, (x + dx) % side

    def device(dy, dx):
        to_y, to_x = chip_at(dy, dx)
        return ((to_y * side + to_x) * CORES + core, z)

    def above(dz):
        return (place, (z + dz) % planes)

    sibling = (place + 1 - 2 * core, z)
    around = [(dy, dx) for dy in range(side) for dx in range(side) if (dy, dx) != (0, 0)]

    group = half // 3
    loads = []
    for at in range(prior // group):
        for step in range(steps):
            blocks = pl.ds(at * group, group)
            loads.append(
                pltpu.make_async_copy(
                    factor.at[step, blocks], tiles.at[step, blocks], load_sem.at[len(loads)]
                )
            )
    extra = [
        pltpu.make_async_copy(factor.at[1, prior], corner, load_sem.at[len(loads)]),
        pltpu.make_async_copy(inverses, inverse, load_sem.at[len(loads) + 1]),
    ]
    for copy in loads + extra:
        copy.start()

    barrier = pltpu.get_barrier_semaphore()
    for dy, dx in around:
        pl.semaphore_signal(barrier, inc=1, device_id=device(dy, dx), device_id_type=MESH)
    for dz in range(1, planes):
        pl.semaphore_signal(barrier, inc=1, device_id=above(dz), device_id_type=MESH)
    pl.semaphore_signal(barrier, inc=1, device_id=sibling, device_id_type=MESH)

    outer, inner = (y, x), (x, y)
    for part in range(2):
        for block in range(half):
            rows_of = earlier[part * half + block]
            known[part, core, outer[part], inner[part], block] = jnp.concatenate(
                [rows_of[0:8], rows_of[8:16]], axis=1
            )

    pl.semaphore_wait(barrier, len(around) + planes)

    def ring(part, distance):
        return device(0, distance) if part == 0 else device(distance, 0)

    def across(part, distance):
        return device(distance, 0) if part == 0 else device(0, distance)

    def remote(source, target, send, recv, to):
        return pltpu.make_async_remote_copy(
            src_ref=source, dst_ref=target, send_sem=send, recv_sem=recv, device_id=to, device_id_type=MESH
        )

    def piece(part, distance):
        return known.at[part, core, outer[part], (inner[part] + distance) % side]

    def whole(part, distance):
        return known.at[part, core, (outer[part] + distance) % side]

    order = [d for d in (2, 1, 3) if d < side]
    for distance in order:
        for part in range(2):
            own = piece(part, 0)
            remote(own, own, send_sem.at[0], ring_sem.at[part, distance], ring(part, distance)).start()

    def forward(part, held):
        own = piece(part, held)
        for distance in order:
            remote(own, own, send_sem.at[1], group_sem.at[part, distance], across(part, distance)).start()

    for part in range(2):
        forward(part, 0)

    def cut(at):
        for step in range(steps):
            loads[at * steps + step].wait()

        def one(block, carry):
            for step in range(steps):
                high, low = split(tiles[step, block])
                tiles_split[block, pl.ds(2 * step * rows, rows)] = high
                tiles_split[block, pl.ds((2 * step + 1) * rows, rows)] = low
            return carry

        lax.fori_loop(at * group, (at + 1) * group, one, 0)

    cut(0)
    cut(1)
    for distance in [d for d in (1, 3, 2) if d < side]:
        for part in range(2):
            at = side - distance
            own = piece(part, at)
            remote(own, own, send_sem.at[0], ring_sem.at[part, distance], ring(part, distance)).wait_recv()
            forward(part, at)
    for part in range(2):
        own = whole(part, 0)
        remote(own, own, send_sem.at[2], core_sem.at[part, 0], sibling).start()
    for at in range(2, prior // group):
        cut(at)

    for copy in extra:
        copy.wait()
    for step in range(steps):
        high, low = split(jnp.transpose(inverse[step]))
        inverse_split[step, 0, 0:rows] = high
        inverse_split[step, 0, rows : 2 * rows] = high
        inverse_split[step, 1, 0:rows] = low
        inverse_split[step, 1, rows : 2 * rows] = low
    high, low = split(jnp.transpose(corner[...]))
    corner_split[:, 0:rows] = high
    corner_split[:, rows : 2 * rows] = low

    for distance in [d for d in (1, 3, 2) if d < side]:
        for part in range(2):
            own = whole(part, side - distance)
            remote(own, own, send_sem.at[1], group_sem.at[part, distance], across(part, distance)).wait_recv()
            remote(own, own, send_sem.at[2], core_sem.at[part, distance], sibling).start()
    for distance in range(side):
        for part in range(2):
            own = whole(part, distance)
            remote(own, own, send_sem.at[2], core_sem.at[part, distance], sibling).wait_recv()

    left = lax.broadcasted_iota(jnp.int32, (8, 2 * outs), 1) < outs

    def unpack(packed):
        high = packed.astype(BF16).astype(F32)
        low = packed - high
        first = jnp.where(left, high, pltpu.roll(low, outs, 1))
        second = jnp.where(left, pltpu.roll(high, outs, 1), low)
        return [first, second]

    sums[...] = jnp.zeros_like(sums)
    for part in range(2):

        def block_sum(block, carry, part=part):
            lines = []
            for at_y in range(side):
                for at_x in range(side):
                    for at_core in range(CORES):
                        at = (at_y, at_x) if part == 0 else (at_x, at_y)
                        lines += unpack(known[part, at_core, at[0], at[1], block])
            weights = jnp.concatenate(lines, axis=0).astype(BF16)
            sums[...] += product(tiles_split[part * half + block], weights)
            return carry

        lax.fori_loop(0, half, block_sum, 0)

    def folded(step):
        both = sums[2 * step * rows : (2 * step + 1) * rows] + sums[(2 * step + 1) * rows : (2 * step + 2) * rows]
        turned = jnp.transpose(both)
        return turned[0:outs] + turned[outs : 2 * outs]

    lanes = parts.shape[-1]
    across_lanes = width // lanes

    for step in range(steps):
        partial = folded(step)
        if step > 0:
            last = jnp.concatenate(
                [
                    jnp.concatenate(
                        [value[step - 1, q * across_lanes + l] for l in range(across_lanes)], axis=1
                    )
                    for q in range(chips // across_lanes)
                ],
                axis=0,
            )
            solved[step - 1] = last
            high, low = split(last)
            update = product(jnp.concatenate([high, low], axis=0), corner_split[...])
            update = update[:, 0:rows] + update[:, rows : 2 * rows]
            partial = partial + (update[0:outs] + update[outs : 2 * outs])
        mine[step] = partial
        for dz in [d for d in (4, 3, 5, 2, 6, 1, 7) if d < planes]:
            remote(mine.at[step], others.at[step, dz - 1], send_sem.at[3 + step], z_sem.at[step], above(dz)).start()
        got = others.at[step]
        remote(got, got, send_sem.at[3 + step], z_sem.at[step], sibling).wait_recv()
        total = partial
        for dz in range(planes - 1):
            total = total + others[step, dz]
        high, low = split(right_side[step] - total)
        both = jnp.concatenate([high, low], axis=1)
        result = product(both, inverse_split[step, 0]) + product(both, inverse_split[step, 1])
        for q in range(chips // across_lanes):
            for l in range(across_lanes):
                term[step, q * across_lanes + l] = result[8 * q : 8 * q + 8, l * lanes : (l + 1) * lanes]
        for at, (dy, dx) in enumerate(around):
            to_y, to_x = chip_at(dy, dx)
            remote(
                term.at[step, to_y * side + to_x], parts.at[step, at], send_sem.at[5 + step], scatter_sem.at[step], device(dy, dx)
            ).start()
        got = parts.at[step]
        remote(got, got, send_sem.at[5 + step], scatter_sem.at[step], sibling).wait_recv()
        here = y * side + x
        total = term[step, here]
        for at in range(chips - 1):
            total = total + parts[step, at]
        pair[step, 0] = total
        swap = remote(pair.at[step, 0], pair.at[step, 1], send_sem.at[7 + step], pair_sem.at[step], sibling)
        swap.start()
        swap.wait_recv()
        value[step, here] = total + pair[step, 1]
        for dy, dx in around:
            remote(value.at[step, here], value.at[step, here], send_sem.at[9 + step], gather_sem.at[step], device(dy, dx)).start()
        got = value.at[step, pl.ds(0, chips - 1)]
        remote(got, got, send_sem.at[9 + step], gather_sem.at[step], sibling).wait_recv()

    step = steps - 1
    for q in range(chips // across_lanes):
        for l in range(across_lanes):
            solved[step, 8 * q : 8 * q + 8, l * lanes : (l + 1) * lanes] = value[step, q * across_lanes + l]

    for part in range(2):
        got = known.at[part, 0, 0, pl.ds(0, side - 1)]
        remote(got, got, send_sem.at[0], ring_sem.at[part, 1], sibling).wait_send()
        got = known.at[part, 0, pl.ds(0, side - 1)]
        remote(got, got, send_sem.at[1], ring_sem.at[part, 1], sibling).wait_send()
        got = known.at[part, 0]
        remote(got, got, send_sem.at[2], ring_sem.at[part, 1], sibling).wait_send()
    for step in range(steps):
        for at, got in (
            (3, others.at[step]),
            (5, parts.at[step]),
            (7, pair.at[step, 0]),
            (9, value.at[step, pl.ds(0, chips - 1)]),
        ):
            remote(got, got, send_sem.at[at + step], z_sem.at[step], sibling).wait_send()


def local(side, planes, factor, inverses, right_side, earlier):
    steps, rows, _, width = factor.shape
    prior, share, outs = earlier.shape
    half = prior // 2
    chips = side * side
    lanes = width * outs // (chips * 8)
    dma, vmem = pltpu.SemaphoreType.DMA, pltpu.VMEM
    any_space = pl.BlockSpec(memory_space=pl.ANY)
    in_vmem = pl.BlockSpec(memory_space=pltpu.VMEM)
    solved = pl.pallas_call(
        functools.partial(kernel, side, planes),
        name="falkon",
        out_shape=jax.ShapeDtypeStruct((steps, outs, width), F32),
        in_specs=[any_space, any_space, in_vmem, in_vmem],
        out_specs=in_vmem,
        scratch_shapes=[
            vmem((2, CORES, side, side, half, 8, 2 * outs), F32),
            vmem((steps, prior, rows, width), F32),
            vmem((prior, 2 * steps * rows, width), BF16),
            vmem((rows, width), F32),
            vmem((steps, width, rows), F32),
            vmem((steps, 2, 2 * rows, width), BF16),
            vmem((width, 2 * rows), BF16),
            vmem((2 * steps * rows, 2 * outs), F32),
            vmem((steps, outs, rows), F32),
            vmem((steps, planes - 1, outs, rows), F32),
            vmem((steps, chips, 8, lanes), F32),
            vmem((steps, chips - 1, 8, lanes), F32),
            vmem((steps, 2, 8, lanes), F32),
            vmem((steps, chips, 8, lanes), F32),
            dma((6 * steps + 2,)),
            dma((11,)),
            dma((2, side)),
            dma((2, side)),
            dma((2, side)),
            dma((steps,)),
            dma((steps,)),
            dma((steps,)),
            dma((steps,)),
        ],
        compiler_params=pltpu.CompilerParams(
            collective_id=0, has_side_effects=True, vmem_limit_bytes=48 << 20
        ),
    )(
        jnp.transpose(factor, (0, 2, 1, 3)),
        inverses,
        jnp.transpose(right_side, (0, 2, 1)),
        earlier,
    )
    return jnp.transpose(solved, (0, 2, 1))


def solution(mesh):
    side = 1
    while side * side * CORES < mesh.shape["row"]:
        side += 1
    in_specs = (
        P(None, "row", None, "col"),
        P(None, "col", "row"),
        P(None, "row", None),
        P(None, ("col", "row"), None),
    )
    return jax.shard_map(
        functools.partial(local, side, mesh.shape["col"]),
        mesh=mesh,
        in_specs=in_specs,
        out_specs=P(None, "col", None),
        check_vma=False,
    )
```

```python
import functools

import jax
import jax.numpy as jnp
from jax import lax
from jax.experimental import pallas as pl
from jax.experimental.pallas import tpu as pltpu
from jax.sharding import PartitionSpec as P

MESH = pl.DeviceIdType.MESH
F32 = jnp.float32
BF16 = jnp.bfloat16
CORES = 2
HALVES = 2
CHUNKS = (((0, 1, 4), (2, 3)), ((5,), (7,)), ((6,), (8,)))


def split(value):
    high = value.astype(BF16)
    return high, (value - high.astype(F32)).astype(BF16)


def product(left, right):
    return jnp.dot(left, right, preferred_element_type=F32)


def kernel(
    side, planes, factor, inverses, right_side, earlier, solved,
    known_00, known_01, known_10, known_11, known_20, known_21, weights, tiles, tiles_split, corner, inverse, inverse_split, corner_split,
    right, early, mine, others, term, parts, value,
    load_sem, ring_send, group_send, core_send, ring_sem, group_sem, core_sem,
    z_send, z_sem, first_send, first_sem, second_send, second_sem,
):
    known = ((known_00, known_01), (known_10, known_11), (known_20, known_21))
    steps, prior, rows, width = tiles.shape
    outs = right_side.shape[1]
    outs_half = outs // HALVES
    place = lax.axis_index("row")
    z = lax.axis_index("col")
    y, x, core = place // (side * CORES), (place // CORES) % side, place % CORES

    def device(dy, dx, other=0):
        to_core = core + other * (1 - 2 * core)
        return (((y + dy) % side * side + (x + dx) % side) * CORES + to_core, z)

    def above(dz):
        return (place, (z + dz) % planes)

    sibling = (place + 1 - 2 * core, z)
    far_ring = [2, 1, 3]
    near_first = [1, 3, 2]
    greeted = [(d * turn, d * (1 - turn), other) for d in far_ring for turn in (0, 1) for other in (0, 1)]
    z_far_first = sorted(range(1, planes), key=lambda d: -min(d, planes - d))

    barrier = pltpu.get_barrier_semaphore()
    for dz in z_far_first:
        pl.semaphore_signal(barrier, inc=1, device_id=above(dz), device_id_type=MESH)
    for place_of in greeted:
        pl.semaphore_signal(barrier, inc=1, device_id=device(*place_of), device_id_type=MESH)
    pl.semaphore_signal(barrier, inc=1, device_id=sibling, device_id_type=MESH)

    copies = []

    def load(source, target):
        copy = pltpu.make_async_copy(source, target, load_sem.at[len(copies)])
        copy.start()
        copies.append(copy)
        return copy

    load_early = load(earlier, early)
    group = 3
    load_tiles = [[], []]

    def load_step(step):
        for at in range(prior // group):
            blocks = pl.ds(at * group, group)
            load_tiles[step].append(load(factor.at[step, blocks], tiles.at[step, blocks]))

    load_step(0)
    load_right = load(right_side, right)
    load_inverse = load(inverses, inverse)
    load_corner = load(factor.at[1, prior], corner)
    load_step(1)

    turns = [(part + core) % 2 for part in range(2)]
    outer = [y * (1 - turn) + x * turn for turn in turns]
    inner = [x * (1 - turn) + y * turn for turn in turns]
    load_early.wait()
    for chunk, parts_of in enumerate(CHUNKS):
        for part, units in enumerate(parts_of):
            for at, unit in enumerate(units):
                if unit == 4:
                    pieces = [early[16], early[17]]
                else:
                    first = 4 * (unit % 5)
                    columns = slice(0, outs_half) if unit < 4 else slice(outs_half, outs)
                    pieces = [early[first + block, :, columns] for block in range(4)]
                known[chunk][part][core, outer[part], inner[part], at] = jnp.concatenate(pieces, axis=1)

    pl.semaphore_wait(barrier, len(greeted) + planes)

    def ring(part, distance):
        return device(distance * turns[part], distance * (1 - turns[part]))

    def across(part, distance):
        return device(distance * (1 - turns[part]), distance * turns[part])

    def remote(source, target, send, recv, to):
        return pltpu.make_async_remote_copy(
            src_ref=source, dst_ref=target, send_sem=send, recv_sem=recv, device_id=to, device_id_type=MESH
        )

    def piece(chunk, part, distance):
        return known[chunk][part].at[core, outer[part], (inner[part] + distance) % side]

    def whole(chunk, part, distance):
        return known[chunk][part].at[core, (outer[part] + distance) % side]

    def whole_other(chunk, part, distance):
        return known[chunk][part].at[1 - core, (inner[part] + distance) % side]

    def go_round(chunk, part, distance):
        own = piece(chunk, part, 0)
        return remote(own, own, ring_send.at[chunk], ring_sem.at[chunk, part, distance], ring(part, distance))

    def go_across(chunk, part, held, distance):
        own = piece(chunk, part, held)
        return remote(own, own, group_send.at[chunk], group_sem.at[chunk, part, distance], across(part, distance))

    def go_over(chunk, part, distance):
        own = whole(chunk, part, distance)
        return remote(own, own, core_send.at[chunk], core_sem.at[chunk, part, distance], sibling)

    chunks = range(len(CHUNKS))

    def drain():
        for chunk in chunks:
            for part in range(2):
                for sent, got in (
                    (ring_send, known[chunk][part].at[0, 0, pl.ds(0, side - 1)]),
                    (group_send, known[chunk][part].at[0, pl.ds(0, side - 1)]),
                    (core_send, known[chunk][part].at[0]),
                ):
                    remote(got, got, sent.at[chunk], ring_sem.at[0, 0, 0], sibling).wait_send()
        for step in range(steps):
            for half in range(HALVES):
                got = others.at[step, half]
                remote(got, got, z_send.at[step, half], z_sem.at[step, half], sibling).wait_send()
                for way in range(2):
                    got = parts.at[step, half, way, pl.ds(0, CORES * side - 1)]
                    remote(got, got, first_send.at[step, half, way], z_sem.at[step, half], sibling).wait_send()
                    remote(got, got, second_send.at[step, half, way], z_sem.at[step, half], sibling).wait_send()

    for chunk in chunks:
        for distance in far_ring:
            for part in range(2):
                go_round(chunk, part, distance).start()
        for distance in far_ring:
            for part in range(2):
                go_across(chunk, part, 0, distance).start()

    def cut(step, at):
        load_tiles[step][at].wait()

        def one(block, carry):
            high, low = split(tiles[step, block])
            tiles_split[step, block, 0:rows] = high
            tiles_split[step, block, rows : 2 * rows] = low
            return carry

        lax.fori_loop(at * group, (at + 1) * group, one, 0)

    lane = lax.broadcasted_iota(jnp.int32, (rows, 128), 1)

    def unpack(chunk, part, distance, other):
        at_outer = ((inner if other else outer)[part] + distance) % side
        turn = 1 - turns[part] if other else turns[part]
        at_core = 1 - core if other else core
        for at_inner in range(side):
            at_y, at_x = at_outer * (1 - turn) + at_inner * turn, at_inner * (1 - turn) + at_outer * turn
            row = pl.multiple_of(((at_y * side + at_x) * CORES + at_core) * 16, 16)
            for at, unit in enumerate(CHUNKS[chunk][part]):
                high, low = split(known[chunk][part][at_core, at_outer, at_inner, at])
                weights[unit, pl.ds(row, 16), 0:128] = high
                weights[unit, pl.ds(row, 16), 128:256] = low

    def ring_in(chunk):
        for distance in near_first:
            for part in range(2):
                go_round(chunk, part, distance).wait_recv()
                for onward in far_ring:
                    go_across(chunk, part, side - distance, onward).start()
        for part in range(2):
            go_over(chunk, part, 0).start()

    def across_in(chunk):
        for part in range(2):
            unpack(chunk, part, 0, False)
        for distance in near_first:
            for part in range(2):
                got = whole(chunk, part, side - distance)
                remote(got, got, group_send.at[chunk], group_sem.at[chunk, part, distance], sibling).wait_recv()
                go_over(chunk, part, side - distance).start()
                unpack(chunk, part, side - distance, False)

    def over_in(chunk):
        for distance in [0] + near_first:
            for part in range(2):
                got = whole_other(chunk, part, distance)
                remote(got, got, core_send.at[chunk], core_sem.at[chunk, part, distance], sibling).wait_recv()
                unpack(chunk, part, distance, True)

    def multiply(step, units):
        total = None
        for unit in units:
            first = 4 * (unit % 5)
            left = tiles_split[step, first : first + 4].reshape(4 * 2 * rows, width)
            term_of = product(left, weights[unit])
            total = term_of if total is None else total + term_of
        found = None
        for block in reversed(range(4)):
            at = 2 * rows * block
            both = total[at : at + rows] + total[at + rows : at + 2 * rows]
            both = both[:, 0:128] + both[:, 128:256]
            found = both if found is None else jnp.where(lane < outs_half * (block + 1), both, found)
        turned = jnp.transpose(found)
        return (turned[0:32] + turned[32:64]) + (turned[64:96] + turned[96:128])

    def multiply_last(step):
        total = product(tiles_split[step, 16:18].reshape(2 * 2 * rows, width), weights[4])
        found = None
        for block in reversed(range(2)):
            at = 2 * rows * block
            both = total[at : at + rows] + total[at + rows : at + 2 * rows]
            both = both[:, 0:128] + both[:, 128:256]
            found = both if found is None else jnp.where(lane < outs, both, found)
        turned = jnp.transpose(found)
        return turned[0:outs] + turned[outs : 2 * outs]

    def send_up(step, half, part_sum):
        mine[step, half] = part_sum
        for dz in z_far_first:
            remote(
                mine.at[step, half], others.at[step, half, dz - 1], z_send.at[step, half], z_sem.at[step, half], above(dz)
            ).start()

    all_loads = prior // group
    cut(0, 0)
    cut(0, 1)
    ring_in(0)
    cut(0, 2)
    cut(0, 3)
    ring_in(1)
    ring_in(2)
    cut(0, 4)
    cut(0, 5)

    load_inverse.wait()
    for step in range(steps):
        high, low = split(jnp.transpose(inverse[step]))
        inverse_split[step, 0, 0:rows] = high
        inverse_split[step, 0, rows : 2 * rows] = high
        inverse_split[step, 1, 0:rows] = low
        inverse_split[step, 1, rows : 2 * rows] = low
    load_corner.wait()
    high, low = split(jnp.transpose(corner[...]))
    corner_split[:, 0:rows] = high
    corner_split[:, rows : 2 * rows] = low

    across_in(0)
    over_in(0)
    last_two = multiply_last(0)
    send_up(0, 0, multiply(0, (0, 1, 2, 3)) + last_two[0:outs_half])
    across_in(1)
    across_in(2)
    over_in(1)
    partial = multiply(0, (5, 7)) + last_two[outs_half:outs]
    over_in(2)
    send_up(0, 1, partial + multiply(0, (6, 8)))

    coordinates = (x, y)
    groups = range(width // 128)

    def along(way, distance, other):
        return device(distance * way, distance * (1 - way), other)

    def take_planes(step, half):
        got = others.at[step, half]
        remote(got, got, z_send.at[step, half], z_sem.at[step, half], sibling).wait_recv()
        total = mine[step, half]
        for dz in range(planes - 1):
            total = total + others[step, half, dz]
        high, low = split(right[step, half * outs_half : (half + 1) * outs_half] - total)
        both = jnp.concatenate([high, low], axis=1)
        result = product(both, inverse_split[step, 0]) + product(both, inverse_split[step, 1])
        for at in groups:
            term[step, half, at] = result[:, 128 * at : 128 * at + 128]
        for way in range(2):
            slot = CORES * coordinates[way] + core
            parts[step, half, way, slot] = term[step, half, 2 * way + core]
            for distance in far_ring + [0]:
                for other in (0, 1) if distance else (1,):
                    remote(
                        term.at[step, half, 2 * way + core + other * (1 - 2 * core)], parts.at[step, half, way, slot],
                        first_send.at[step, half, way], first_sem.at[step, half, way], along(way, distance, other),
                    ).start()

    def take_first(step, half):
        for way in range(2):
            got = parts.at[step, half, way, pl.ds(0, CORES * side - 1)]
            remote(got, got, first_send.at[step, half, way], first_sem.at[step, half, way], sibling).wait_recv()
            total = parts[step, half, way, 0]
            for slot in range(1, CORES * side):
                total = total + parts[step, half, way, slot]
            slot = coordinates[1 - way]
            value[step, half, 2 * way + core, slot] = total
            own = value.at[step, half, 2 * way + core, slot]
            for distance in far_ring + [0]:
                for other in (0, 1) if distance else (1,):
                    remote(
                        own, own, second_send.at[step, half, way], second_sem.at[step, half, way, other],
                        along(1 - way, distance, other),
                    ).start()

    def take_second(step, half):
        for way in range(2):
            for other in (0, 1):
                got = value.at[step, half, 2 * way, pl.ds(0, side - 1 + other)]
                remote(
                    got, got, second_send.at[step, half, way], second_sem.at[step, half, way, other], sibling
                ).wait_recv()
        last = []
        for at in groups:
            total = value[step, half, at, 0]
            for slot in range(1, side):
                total = total + value[step, half, at, slot]
            last.append(total)
        last = jnp.concatenate(last, axis=1)
        solved[step, half * outs_half : (half + 1) * outs_half] = last
        return last

    load_right.wait()
    for at in range(all_loads):
        cut(1, at)
    later = []
    for step in range(steps):
        take_planes(step, 0)
        if step == 0:
            last_two = multiply_last(1)
            later = [
                multiply(1, range(5 * half, 5 * half + 4)) + last_two[half * outs_half : (half + 1) * outs_half]
                for half in range(HALVES)
            ]
        take_planes(step, 1)
        for half in range(HALVES):
            take_first(step, half)
        for half in range(HALVES):
            last = take_second(step, half)
            if step + 1 < steps:
                high, low = split(last)
                update = product(jnp.concatenate([high, low], axis=0), corner_split[...])
                update = update[:, 0:rows] + update[:, rows : 2 * rows]
                update = update[0:outs_half] + update[outs_half : 2 * outs_half]
                send_up(step + 1, half, later[half] + update)

    drain()


def local(side, planes, factor, inverses, right_side, earlier):
    steps, rows, _, width = factor.shape
    prior, share, outs = earlier.shape
    outs_half = outs // HALVES
    chunks = len(CHUNKS)
    dma, vmem = pltpu.SemaphoreType.DMA, pltpu.VMEM
    in_hbm = pl.BlockSpec(memory_space=pltpu.HBM)
    solved = pl.pallas_call(
        functools.partial(kernel, side, planes),
        name="falkon",
        out_shape=jax.ShapeDtypeStruct((steps, outs, width), F32),
        in_specs=[in_hbm] * 4,
        out_specs=pl.BlockSpec(memory_space=pltpu.VMEM),
        scratch_shapes=[
            *[vmem((CORES, side, side, len(units), 16, 128), F32) for chunk in CHUNKS for units in chunk],
            vmem((9, width, 256), BF16),
            vmem((steps, prior, rows, width), F32),
            vmem((steps, prior, 2 * rows, width), BF16),
            vmem((rows, width), F32),
            vmem((steps, width, rows), F32),
            vmem((steps, 2, 2 * rows, width), BF16),
            vmem((width, 2 * rows), BF16),
            vmem((steps, outs, rows), F32),
            vmem((prior, share, outs), F32),
            vmem((steps, HALVES, outs_half, rows), F32),
            vmem((steps, HALVES, planes - 1, outs_half, rows), F32),
            vmem((steps, HALVES, 2 * CORES, outs_half, 128), F32),
            vmem((steps, HALVES, 2, CORES * side, outs_half, 128), F32),
            vmem((steps, HALVES, 2 * CORES, side, outs_half, 128), F32),
            dma((16,)),
            dma((chunks,)),
            dma((chunks,)),
            dma((chunks,)),
            dma((chunks, 2, side)),
            dma((chunks, 2, side)),
            dma((chunks, 2, side)),
            dma((steps, HALVES)),
            dma((steps, HALVES)),
            dma((steps, HALVES, 2)),
            dma((steps, HALVES, 2)),
            dma((steps, HALVES, 2)),
            dma((steps, HALVES, 2, 2)),
        ],
        compiler_params=pltpu.CompilerParams(
            collective_id=0, has_side_effects=True, vmem_limit_bytes=40 << 20
        ),
    )(
        *[
            pltpu.with_memory_space_constraint(array, pltpu.HBM)
            for array in (
                jnp.transpose(factor, (0, 2, 1, 3)),
                inverses,
                jnp.transpose(right_side, (0, 2, 1)),
                earlier,
            )
        ]
    )
    return jnp.transpose(solved, (0, 2, 1))


def solution(mesh):
    side = 1
    while side * side * CORES < mesh.shape["row"]:
        side += 1
    in_specs = (
        P(None, "row", None, "col"),
        P(None, "col", "row"),
        P(None, "row", None),
        P(None, ("col", "row"), None),
    )
    return jax.shard_map(
        functools.partial(local, side, mesh.shape["col"]),
        mesh=mesh,
        in_specs=in_specs,
        out_specs=P(None, "col", None),
        check_vma=False,
    )
```

```python
import functools

import jax
import jax.numpy as jnp
from jax import lax
from jax.experimental import pallas as pl
from jax.experimental.pallas import tpu as pltpu
from jax.sharding import PartitionSpec as P

MESH = pl.DeviceIdType.MESH
F32 = jnp.float32
BF16 = jnp.bfloat16
CORES = 2
HALVES = 2
CHUNKS = (((0, 1, 4), (2, 3)), ((5,), (7,)), ((6,), (8,)))


def split(value):
    high = value.astype(BF16)
    return high, (value - high.astype(F32)).astype(BF16)


def product(left, right):
    return jnp.dot(left, right, preferred_element_type=F32)


def kernel(
    side, planes, factor, inverses, right_side, earlier, solved,
    known_00, known_01, known_10, known_11, known_20, known_21, weights, tiles, tiles_split, corner, inverse, inverse_split, corner_split,
    right, early, mine, others, term, parts, value,
    load_sem, ring_send, group_send, core_send, ring_sem, group_sem, core_sem,
    z_send, z_sem, first_send, first_sem, second_send, second_sem, vouch_sem,
):
    known = ((known_00, known_01), (known_10, known_11), (known_20, known_21))
    steps, prior, rows, width = tiles.shape
    outs = right_side.shape[1]
    outs_half = outs // HALVES
    place = lax.axis_index("row")
    z = lax.axis_index("col")
    y, x, core = place // (side * CORES), (place // CORES) % side, place % CORES

    def device(dy, dx, other=0):
        to_core = core + other * (1 - 2 * core)
        return (((y + dy) % side * side + (x + dx) % side) * CORES + to_core, z)

    def above(dz):
        return (place, (z + dz) % planes)

    sibling = (place + 1 - 2 * core, z)
    far_ring = [2, 1, 3]
    near_first = [1, 3, 2]
    z_far_first = sorted(range(1, planes), key=lambda d: -min(d, planes - d))

    greeted = [device(d * turn, d * (1 - turn)) for d in far_ring for turn in (0, 1)]
    greeted += [above(dz) for dz in (2, planes - 2, 1, planes - 1)] + [sibling]
    barrier = pltpu.get_barrier_semaphore()
    for to in greeted:
        pl.semaphore_signal(barrier, inc=1, device_id=to, device_id_type=MESH)

    copies = []

    def load(source, target):
        copy = pltpu.make_async_copy(source, target, load_sem.at[len(copies)])
        copy.start()
        copies.append(copy)
        return copy

    load_early = load(earlier, early)
    group = 3
    load_tiles = [[], []]

    def load_step(step):
        for at in range(prior // group):
            blocks = pl.ds(at * group, group)
            load_tiles[step].append(load(factor.at[step, blocks], tiles.at[step, blocks]))

    load_step(0)
    load_right = load(right_side, right)
    load_inverse = load(inverses, inverse)
    load_corner = load(factor.at[1, prior], corner)
    load_step(1)

    turns = [(part + core) % 2 for part in range(2)]
    outer = [y * (1 - turn) + x * turn for turn in turns]
    inner = [x * (1 - turn) + y * turn for turn in turns]
    load_early.wait()
    for chunk, parts_of in enumerate(CHUNKS):
        for part, units in enumerate(parts_of):
            for at, unit in enumerate(units):
                if unit == 4:
                    pieces = [early[16], early[17]]
                else:
                    first = 4 * (unit % 5)
                    columns = slice(0, outs_half) if unit < 4 else slice(outs_half, outs)
                    pieces = [early[first + block, :, columns] for block in range(4)]
                known[chunk][part][core, outer[part], inner[part], at] = jnp.concatenate(pieces, axis=1)

    pl.semaphore_wait(barrier, len(greeted))
    vouched_by = [above(2), above(planes - 2), sibling]
    for to in vouched_by:
        pl.semaphore_signal(vouch_sem, inc=1, device_id=to, device_id_type=MESH)

    def ring(part, distance):
        return device(distance * turns[part], distance * (1 - turns[part]))

    def across(part, distance):
        return device(distance * (1 - turns[part]), distance * turns[part])

    def remote(source, target, send, recv, to):
        return pltpu.make_async_remote_copy(
            src_ref=source, dst_ref=target, send_sem=send, recv_sem=recv, device_id=to, device_id_type=MESH
        )

    def piece(chunk, part, distance):
        return known[chunk][part].at[core, outer[part], (inner[part] + distance) % side]

    def whole(chunk, part, distance):
        return known[chunk][part].at[core, (outer[part] + distance) % side]

    def whole_other(chunk, part, distance):
        return known[chunk][part].at[1 - core, (inner[part] + distance) % side]

    def go_round(chunk, part, distance):
        own = piece(chunk, part, 0)
        return remote(own, own, ring_send.at[chunk], ring_sem.at[chunk, part, distance], ring(part, distance))

    def go_across(chunk, part, held, distance):
        own = piece(chunk, part, held)
        return remote(own, own, group_send.at[chunk], group_sem.at[chunk, part, distance], across(part, distance))

    def go_over(chunk, part, distance):
        own = whole(chunk, part, distance)
        return remote(own, own, core_send.at[chunk], core_sem.at[chunk, part, distance], sibling)

    chunks = range(len(CHUNKS))

    def drain():
        for chunk in chunks:
            for part in range(2):
                for sent, got in (
                    (ring_send, known[chunk][part].at[0, 0, pl.ds(0, side - 1)]),
                    (group_send, known[chunk][part].at[0, pl.ds(0, side - 1)]),
                    (core_send, known[chunk][part].at[0]),
                ):
                    remote(got, got, sent.at[chunk], ring_sem.at[0, 0, 0], sibling).wait_send()
        for step in range(steps):
            for half in range(HALVES):
                got = others.at[step, half]
                remote(got, got, z_send.at[step, half], z_sem.at[step, half], sibling).wait_send()
                for way in range(2):
                    got = parts.at[step, half, way, pl.ds(0, CORES * side - 1)]
                    remote(got, got, first_send.at[step, half, way], z_sem.at[step, half], sibling).wait_send()
                    remote(got, got, second_send.at[step, half, way], z_sem.at[step, half], sibling).wait_send()

    def ring_out(chunk):
        for distance in far_ring:
            for part in range(2):
                go_round(chunk, part, distance).start()

    def across_out(chunk):
        for distance in far_ring:
            for part in range(2):
                go_across(chunk, part, 0, distance).start()

    def cut(step, at):
        load_tiles[step][at].wait()

        def one(block, carry):
            high, low = split(tiles[step, block])
            tiles_split[step, block, 0:rows] = high
            tiles_split[step, block, rows : 2 * rows] = low
            return carry

        lax.fori_loop(at * group, (at + 1) * group, one, 0)

    lane = lax.broadcasted_iota(jnp.int32, (rows, 128), 1)

    def unpack(chunk, part, distance, other):
        at_outer = ((inner if other else outer)[part] + distance) % side
        turn = 1 - turns[part] if other else turns[part]
        at_core = 1 - core if other else core
        for at_inner in range(side):
            at_y, at_x = at_outer * (1 - turn) + at_inner * turn, at_inner * (1 - turn) + at_outer * turn
            row = pl.multiple_of(((at_y * side + at_x) * CORES + at_core) * 16, 16)
            for at, unit in enumerate(CHUNKS[chunk][part]):
                high, low = split(known[chunk][part][at_core, at_outer, at_inner, at])
                weights[unit, pl.ds(row, 16), 0:128] = high
                weights[unit, pl.ds(row, 16), 128:256] = low

    def ring_in(chunk):
        for distance in near_first:
            for part in range(2):
                go_round(chunk, part, distance).wait_recv()
                for onward in far_ring:
                    go_across(chunk, part, side - distance, onward).start()
        for part in range(2):
            go_over(chunk, part, 0).start()

    def across_in(chunk, distances=(0, *near_first)):
        for distance in distances:
            for part in range(2):
                if distance > 0:
                    got = whole(chunk, part, side - distance)
                    remote(got, got, group_send.at[chunk], group_sem.at[chunk, part, distance], sibling).wait_recv()
                    go_over(chunk, part, side - distance).start()
                unpack(chunk, part, (side - distance) % side, False)

    def over_in(chunk):
        for distance in [0] + near_first:
            for part in range(2):
                got = whole_other(chunk, part, distance)
                remote(got, got, core_send.at[chunk], core_sem.at[chunk, part, distance], sibling).wait_recv()
                unpack(chunk, part, distance, True)

    def multiply(step, units):
        total = None
        for unit in units:
            first = 4 * (unit % 5)
            left = tiles_split[step, first : first + 4].reshape(4 * 2 * rows, width)
            term_of = product(left, weights[unit])
            total = term_of if total is None else total + term_of
        found = None
        for block in reversed(range(4)):
            at = 2 * rows * block
            both = total[at : at + rows] + total[at + rows : at + 2 * rows]
            both = both[:, 0:128] + both[:, 128:256]
            found = both if found is None else jnp.where(lane < outs_half * (block + 1), both, found)
        turned = jnp.transpose(found)
        return (turned[0:32] + turned[32:64]) + (turned[64:96] + turned[96:128])

    def multiply_last(step):
        total = product(tiles_split[step, 16:18].reshape(2 * 2 * rows, width), weights[4])
        found = None
        for block in reversed(range(2)):
            at = 2 * rows * block
            both = total[at : at + rows] + total[at + rows : at + 2 * rows]
            both = both[:, 0:128] + both[:, 128:256]
            found = both if found is None else jnp.where(lane < outs, both, found)
        turned = jnp.transpose(found)
        return turned[0:outs] + turned[outs : 2 * outs]

    def send_up(step, half, part_sum):
        mine[step, half] = part_sum
        for dz in z_far_first:
            remote(
                mine.at[step, half], others.at[step, half, dz - 1], z_send.at[step, half], z_sem.at[step, half], above(dz)
            ).start()

    def prepare():
        load_inverse.wait()
        for step in range(steps):
            high, low = split(jnp.transpose(inverse[step]))
            inverse_split[step, 0, 0:rows] = high
            inverse_split[step, 0, rows : 2 * rows] = high
            inverse_split[step, 1, 0:rows] = low
            inverse_split[step, 1, rows : 2 * rows] = low
        load_corner.wait()
        high, low = split(jnp.transpose(corner[...]))
        corner_split[:, 0:rows] = high
        corner_split[:, rows : 2 * rows] = low

    all_loads = prior // group
    ring_out(0)
    across_out(0)
    ring_out(1)
    ring_out(2)
    cut(0, 0)
    cut(0, 1)
    ring_in(0)
    across_out(1)
    cut(0, 2)
    cut(0, 3)
    cut(0, 4)
    cut(0, 5)
    prepare()
    ring_in(1)
    across_in(0, (0, 1))
    across_out(2)
    ring_in(2)
    across_in(0, (3, 2))
    over_in(0)
    pl.semaphore_wait(vouch_sem, len(vouched_by))
    last_two = multiply_last(0)
    send_up(0, 0, multiply(0, (0, 1, 2, 3)) + last_two[0:outs_half])
    across_in(1)
    across_in(2)
    over_in(1)
    partial = multiply(0, (5, 7)) + last_two[outs_half:outs]
    over_in(2)
    send_up(0, 1, partial + multiply(0, (6, 8)))

    coordinates = (x, y)
    groups = range(width // 128)

    def along(way, distance, other):
        return device(distance * way, distance * (1 - way), other)

    def take_planes(step, half):
        got = others.at[step, half]
        remote(got, got, z_send.at[step, half], z_sem.at[step, half], sibling).wait_recv()
        total = mine[step, half]
        for dz in range(planes - 1):
            total = total + others[step, half, dz]
        high, low = split(right[step, half * outs_half : (half + 1) * outs_half] - total)
        both = jnp.concatenate([high, low], axis=1)
        result = product(both, inverse_split[step, 0]) + product(both, inverse_split[step, 1])
        for at in groups:
            term[step, half, at] = result[:, 128 * at : 128 * at + 128]
        for way in range(2):
            slot = CORES * coordinates[way] + core
            parts[step, half, way, slot] = term[step, half, 2 * way + core]
            for distance in far_ring + [0]:
                for other in (0, 1) if distance else (1,):
                    remote(
                        term.at[step, half, 2 * way + core + other * (1 - 2 * core)], parts.at[step, half, way, slot],
                        first_send.at[step, half, way], first_sem.at[step, half, way], along(way, distance, other),
                    ).start()

    def take_first(step, half):
        for way in range(2):
            got = parts.at[step, half, way, pl.ds(0, CORES * side - 1)]
            remote(got, got, first_send.at[step, half, way], first_sem.at[step, half, way], sibling).wait_recv()
            total = parts[step, half, way, 0]
            for slot in range(1, CORES * side):
                total = total + parts[step, half, way, slot]
            slot = coordinates[1 - way]
            value[step, half, 2 * way + core, slot] = total
            own = value.at[step, half, 2 * way + core, slot]
            for distance in far_ring + [0]:
                for other in (0, 1) if distance else (1,):
                    remote(
                        own, own, second_send.at[step, half, way], second_sem.at[step, half, way, other],
                        along(1 - way, distance, other),
                    ).start()

    def take_second(step, half):
        for way in range(2):
            for other in (0, 1):
                got = value.at[step, half, 2 * way, pl.ds(0, side - 1 + other)]
                remote(
                    got, got, second_send.at[step, half, way], second_sem.at[step, half, way, other], sibling
                ).wait_recv()
        last = []
        for at in groups:
            total = value[step, half, at, 0]
            for slot in range(1, side):
                total = total + value[step, half, at, slot]
            last.append(total)
        last = jnp.concatenate(last, axis=1)
        solved[step, half * outs_half : (half + 1) * outs_half] = last
        return last

    load_right.wait()
    for at in range(all_loads):
        cut(1, at)
    later = []
    for step in range(steps):
        take_planes(step, 0)
        if step == 0:
            last_two = multiply_last(1)
            later = [
                multiply(1, range(5 * half, 5 * half + 4)) + last_two[half * outs_half : (half + 1) * outs_half]
                for half in range(HALVES)
            ]
        take_planes(step, 1)
        for half in range(HALVES):
            take_first(step, half)
        for half in range(HALVES):
            last = take_second(step, half)
            if step + 1 < steps:
                high, low = split(last)
                update = product(jnp.concatenate([high, low], axis=0), corner_split[...])
                update = update[:, 0:rows] + update[:, rows : 2 * rows]
                update = update[0:outs_half] + update[outs_half : 2 * outs_half]
                send_up(step + 1, half, later[half] + update)

    drain()


def local(side, planes, factor, inverses, right_side, earlier):
    steps, rows, _, width = factor.shape
    prior, share, outs = earlier.shape
    outs_half = outs // HALVES
    chunks = len(CHUNKS)
    dma, vmem = pltpu.SemaphoreType.DMA, pltpu.VMEM
    in_hbm = pl.BlockSpec(memory_space=pltpu.HBM)
    solved = pl.pallas_call(
        functools.partial(kernel, side, planes),
        name="falkon",
        out_shape=jax.ShapeDtypeStruct((steps, outs, width), F32),
        in_specs=[in_hbm] * 4,
        out_specs=pl.BlockSpec(memory_space=pltpu.VMEM),
        scratch_shapes=[
            *[vmem((CORES, side, side, len(units), 16, 128), F32) for chunk in CHUNKS for units in chunk],
            vmem((9, width, 256), BF16),
            vmem((steps, prior, rows, width), F32),
            vmem((steps, prior, 2 * rows, width), BF16),
            vmem((rows, width), F32),
            vmem((steps, width, rows), F32),
            vmem((steps, 2, 2 * rows, width), BF16),
            vmem((width, 2 * rows), BF16),
            vmem((steps, outs, rows), F32),
            vmem((prior, share, outs), F32),
            vmem((steps, HALVES, outs_half, rows), F32),
            vmem((steps, HALVES, planes - 1, outs_half, rows), F32),
            vmem((steps, HALVES, 2 * CORES, outs_half, 128), F32),
            vmem((steps, HALVES, 2, CORES * side, outs_half, 128), F32),
            vmem((steps, HALVES, 2 * CORES, side, outs_half, 128), F32),
            dma((16,)),
            dma((chunks,)),
            dma((chunks,)),
            dma((chunks,)),
            dma((chunks, 2, side)),
            dma((chunks, 2, side)),
            dma((chunks, 2, side)),
            dma((steps, HALVES)),
            dma((steps, HALVES)),
            dma((steps, HALVES, 2)),
            dma((steps, HALVES, 2)),
            dma((steps, HALVES, 2)),
            dma((steps, HALVES, 2, 2)),
            pltpu.SemaphoreType.REGULAR,
        ],
        compiler_params=pltpu.CompilerParams(
            collective_id=0, has_side_effects=True, vmem_limit_bytes=40 << 20
        ),
    )(
        *[
            pltpu.with_memory_space_constraint(array, pltpu.HBM)
            for array in (
                jnp.transpose(factor, (0, 2, 1, 3)),
                inverses,
                jnp.transpose(right_side, (0, 2, 1)),
                earlier,
            )
        ]
    )
    return jnp.transpose(solved, (0, 2, 1))


def solution(mesh):
    side = 1
    while side * side * CORES < mesh.shape["row"]:
        side += 1
    in_specs = (
        P(None, "row", None, "col"),
        P(None, "col", "row"),
        P(None, "row", None),
        P(None, ("col", "row"), None),
    )
    return jax.shard_map(
        functools.partial(local, side, mesh.shape["col"]),
        mesh=mesh,
        in_specs=in_specs,
        out_specs=P(None, "col", None),
        check_vma=False,
    )
```

```python
import functools

import jax
import jax.numpy as jnp
from jax import lax
from jax.experimental import pallas as pl
from jax.experimental.pallas import tpu as pltpu
from jax.sharding import PartitionSpec as P

MESH = pl.DeviceIdType.MESH
F32 = jnp.float32
BF16 = jnp.bfloat16
CORES = 2
HALVES = 2
CHUNKS = (((0, 1, 4), (2, 3)), ((5,), (7,)), ((6,), (8,)))


def split(value):
    high = value.astype(BF16)
    return high, (value - high.astype(F32)).astype(BF16)


def product(left, right):
    return jnp.dot(left, right, preferred_element_type=F32)


def kernel(
    side, planes, factor, inverses, right_side, earlier, solved,
    known_00, known_01, known_10, known_11, known_20, known_21, weights, tiles, tiles_split, corner, inverse, inverse_split, corner_split,
    right, early, mine, others, term, parts, value,
    load_sem, ring_send, group_send, core_send, ring_sem, group_sem, core_sem,
    z_send, z_sem, first_send, first_sem, second_send, second_sem, vouch_sem,
):
    known = ((known_00, known_01), (known_10, known_11), (known_20, known_21))
    steps, prior, rows, width = tiles.shape
    outs = right_side.shape[1]
    outs_half = outs // HALVES
    place = lax.axis_index("row")
    z = lax.axis_index("col")
    y, x, core = place // (side * CORES), (place // CORES) % side, place % CORES

    def device(dy, dx, other=0):
        to_core = core + other * (1 - 2 * core)
        return (((y + dy) % side * side + (x + dx) % side) * CORES + to_core, z)

    def above(dz):
        return (place, (z + dz) % planes)

    sibling = (place + 1 - 2 * core, z)
    far_ring = [2, 1, 3]
    near_first = [1, 3, 2]
    z_far_first = sorted(range(1, planes), key=lambda d: -min(d, planes - d))

    greeted = [device(d * turn, d * (1 - turn)) for d in far_ring for turn in (0, 1)]
    greeted += [above(dz) for dz in (2, planes - 2, 1, planes - 1)] + [sibling]
    barrier = pltpu.get_barrier_semaphore()
    for to in greeted:
        pl.semaphore_signal(barrier, inc=1, device_id=to, device_id_type=MESH)

    copies = []

    def load(source, target):
        copy = pltpu.make_async_copy(source, target, load_sem.at[len(copies)])
        copy.start()
        copies.append(copy)
        return copy

    load_early = load(earlier, early)
    group = 3
    load_tiles = [[], []]

    def load_step(step):
        for at in range(prior // group):
            blocks = pl.ds(at * group, group)
            load_tiles[step].append(load(factor.at[step, blocks], tiles.at[step, blocks]))

    load_step(0)
    load_right = load(right_side, right)
    load_inverse = load(inverses, inverse)
    load_corner = load(factor.at[1, prior], corner)
    load_step(1)

    turns = [(part + core) % 2 for part in range(2)]
    outer = [y * (1 - turn) + x * turn for turn in turns]
    inner = [x * (1 - turn) + y * turn for turn in turns]
    load_early.wait()
    for chunk, parts_of in enumerate(CHUNKS):
        for part, units in enumerate(parts_of):
            for at, unit in enumerate(units):
                if unit == 4:
                    pieces = [early[16], early[17]]
                else:
                    first = 4 * (unit % 5)
                    columns = slice(0, outs_half) if unit < 4 else slice(outs_half, outs)
                    pieces = [early[first + block, :, columns] for block in range(4)]
                known[chunk][part][core, outer[part], inner[part], at] = jnp.concatenate(pieces, axis=1)

    pl.semaphore_wait(barrier, len(greeted))
    vouched_by = [above(2), above(planes - 2), sibling]
    for to in vouched_by:
        pl.semaphore_signal(vouch_sem, inc=1, device_id=to, device_id_type=MESH)

    def ring(part, distance):
        return device(distance * turns[part], distance * (1 - turns[part]))

    def across(part, distance):
        return device(distance * (1 - turns[part]), distance * turns[part])

    def remote(source, target, send, recv, to):
        return pltpu.make_async_remote_copy(
            src_ref=source, dst_ref=target, send_sem=send, recv_sem=recv, device_id=to, device_id_type=MESH
        )

    def piece(chunk, part, distance):
        return known[chunk][part].at[core, outer[part], (inner[part] + distance) % side]

    def whole(chunk, part, distance):
        return known[chunk][part].at[core, (outer[part] + distance) % side]

    def whole_other(chunk, part, distance):
        return known[chunk][part].at[1 - core, (inner[part] + distance) % side]

    def go_round(chunk, part, distance):
        own = piece(chunk, part, 0)
        return remote(own, own, ring_send.at[chunk], ring_sem.at[chunk, part, distance], ring(part, distance))

    def go_across(chunk, part, held, distance):
        own = piece(chunk, part, held)
        return remote(own, own, group_send.at[chunk], group_sem.at[chunk, part, distance], across(part, distance))

    def go_over(chunk, part, distance):
        own = whole(chunk, part, distance)
        return remote(own, own, core_send.at[chunk], core_sem.at[chunk, part, distance], sibling)

    chunks = range(len(CHUNKS))

    def drain():
        for chunk in chunks:
            for part in range(2):
                for sent, got in (
                    (ring_send, known[chunk][part].at[0, 0, pl.ds(0, side - 1)]),
                    (group_send, known[chunk][part].at[0, pl.ds(0, side - 1)]),
                    (core_send, known[chunk][part].at[0]),
                ):
                    remote(got, got, sent.at[chunk], ring_sem.at[0, 0, 0], sibling).wait_send()
        for step in range(steps):
            for half in range(HALVES):
                got = others.at[step, half]
                remote(got, got, z_send.at[step, half], z_sem.at[step, half], sibling).wait_send()
                for way in range(2):
                    got = parts.at[step, half, way, pl.ds(0, CORES * side - 1)]
                    remote(got, got, first_send.at[step, half, way], z_sem.at[step, half], sibling).wait_send()
                    remote(got, got, second_send.at[step, half, way], z_sem.at[step, half], sibling).wait_send()

    def ring_out(chunk):
        for distance in far_ring:
            for part in range(2):
                go_round(chunk, part, distance).start()

    def across_out(chunk):
        for distance in far_ring:
            for part in range(2):
                go_across(chunk, part, 0, distance).start()

    def cut(step, at):
        load_tiles[step][at].wait()

        def one(block, carry):
            high, low = split(tiles[step, block])
            tiles_split[step, block, 0:rows] = high
            tiles_split[step, block, rows : 2 * rows] = low
            return carry

        lax.fori_loop(at * group, (at + 1) * group, one, 0)

    lane = lax.broadcasted_iota(jnp.int32, (rows, 128), 1)

    def unpack(chunk, part, distance, other):
        at_outer = ((inner if other else outer)[part] + distance) % side
        turn = 1 - turns[part] if other else turns[part]
        at_core = 1 - core if other else core
        for at_inner in range(side):
            at_y, at_x = at_outer * (1 - turn) + at_inner * turn, at_inner * (1 - turn) + at_outer * turn
            row = pl.multiple_of(((at_y * side + at_x) * CORES + at_core) * 16, 16)
            for at, unit in enumerate(CHUNKS[chunk][part]):
                high, low = split(known[chunk][part][at_core, at_outer, at_inner, at])
                weights[unit, pl.ds(row, 16), 0:128] = high
                weights[unit, pl.ds(row, 16), 128:256] = low

    def ring_in(chunk):
        for distance in near_first:
            for part in range(2):
                go_round(chunk, part, distance).wait_recv()
                for onward in far_ring:
                    go_across(chunk, part, side - distance, onward).start()
        for part in range(2):
            go_over(chunk, part, 0).start()

    def across_in(chunk, distances=(0, *near_first)):
        for distance in distances:
            for part in range(2):
                if distance > 0:
                    got = whole(chunk, part, side - distance)
                    remote(got, got, group_send.at[chunk], group_sem.at[chunk, part, distance], sibling).wait_recv()
                    go_over(chunk, part, side - distance).start()
                unpack(chunk, part, (side - distance) % side, False)

    def over_in(chunk):
        for distance in [0] + near_first:
            for part in range(2):
                got = whole_other(chunk, part, distance)
                remote(got, got, core_send.at[chunk], core_sem.at[chunk, part, distance], sibling).wait_recv()
                unpack(chunk, part, distance, True)

    def multiply(step, units):
        total = None
        for unit in units:
            first = 4 * (unit % 5)
            left = tiles_split[step, first : first + 4].reshape(4 * 2 * rows, width)
            term_of = product(left, weights[unit])
            total = term_of if total is None else total + term_of
        found = None
        for block in reversed(range(4)):
            at = 2 * rows * block
            both = total[at : at + rows] + total[at + rows : at + 2 * rows]
            both = both[:, 0:128] + both[:, 128:256]
            found = both if found is None else jnp.where(lane < outs_half * (block + 1), both, found)
        turned = jnp.transpose(found)
        return (turned[0:32] + turned[32:64]) + (turned[64:96] + turned[96:128])

    def multiply_last(step):
        total = product(tiles_split[step, 16:18].reshape(2 * 2 * rows, width), weights[4])
        found = None
        for block in reversed(range(2)):
            at = 2 * rows * block
            both = total[at : at + rows] + total[at + rows : at + 2 * rows]
            both = both[:, 0:128] + both[:, 128:256]
            found = both if found is None else jnp.where(lane < outs, both, found)
        turned = jnp.transpose(found)
        return turned[0:outs] + turned[outs : 2 * outs]

    def send_up(step, half, part_sum):
        mine[step, half] = part_sum
        for dz in z_far_first:
            remote(
                mine.at[step, half], others.at[step, half, dz - 1], z_send.at[step, half], z_sem.at[step, half], above(dz)
            ).start()

    def prepare():
        load_inverse.wait()
        for step in range(steps):
            high, low = split(jnp.transpose(inverse[step]))
            inverse_split[step, 0, 0:rows] = high
            inverse_split[step, 0, rows : 2 * rows] = high
            inverse_split[step, 1, 0:rows] = low
            inverse_split[step, 1, rows : 2 * rows] = low
        load_corner.wait()
        high, low = split(jnp.transpose(corner[...]))
        corner_split[:, 0:rows] = high
        corner_split[:, rows : 2 * rows] = low

    all_loads = prior // group
    ring_out(0)
    across_out(0)
    ring_out(1)
    ring_out(2)
    cut(0, 0)
    cut(0, 1)
    ring_in(0)
    across_out(1)
    cut(0, 2)
    cut(0, 3)
    cut(0, 4)
    cut(0, 5)
    prepare()
    ring_in(1)
    across_in(0, (0, 1))
    across_out(2)
    ring_in(2)
    across_in(0, (3, 2))
    over_in(0)
    pl.semaphore_wait(vouch_sem, len(vouched_by))
    last_two = multiply_last(0)
    send_up(0, 0, multiply(0, (0, 1, 2, 3)) + last_two[0:outs_half])
    across_in(1)
    across_in(2)
    over_in(1)
    partial = multiply(0, (5, 7)) + last_two[outs_half:outs]
    over_in(2)
    send_up(0, 1, partial + multiply(0, (6, 8)))

    coordinates = (x, y)
    in_plane = ((2, 1), (2, 0), (1, 1), (3, 1), (1, 0), (3, 0), (0, 1))
    groups = range(width // 128)

    def along(way, distance, other):
        return device(distance * way, distance * (1 - way), other)

    def take_planes(step, half):
        got = others.at[step, half]
        remote(got, got, z_send.at[step, half], z_sem.at[step, half], sibling).wait_recv()
        total = mine[step, half]
        for dz in range(planes - 1):
            total = total + others[step, half, dz]
        high, low = split(right[step, half * outs_half : (half + 1) * outs_half] - total)
        both = jnp.concatenate([high, low], axis=1)
        result = product(both, inverse_split[step, 0]) + product(both, inverse_split[step, 1])
        for at in groups:
            term[step, half, at] = result[:, 128 * at : 128 * at + 128]
        for way in range(2):
            slot = CORES * coordinates[way] + core
            parts[step, half, way, slot] = term[step, half, 2 * way + core]
            for distance, other in in_plane:
                remote(
                    term.at[step, half, 2 * way + core + other * (1 - 2 * core)], parts.at[step, half, way, slot],
                    first_send.at[step, half, way], first_sem.at[step, half, way], along(way, distance, other),
                ).start()

    def take_first(step, half):
        for way in range(2):
            got = parts.at[step, half, way, pl.ds(0, CORES * side - 1)]
            remote(got, got, first_send.at[step, half, way], first_sem.at[step, half, way], sibling).wait_recv()
            total = parts[step, half, way, 0]
            for slot in range(1, CORES * side):
                total = total + parts[step, half, way, slot]
            slot = coordinates[1 - way]
            value[step, half, 2 * way + core, slot] = total
            own = value.at[step, half, 2 * way + core, slot]
            for distance, other in in_plane:
                remote(
                    own, own, second_send.at[step, half, way], second_sem.at[step, half, way, other],
                    along(1 - way, distance, other),
                ).start()

    def take_second(step, half):
        for way in range(2):
            for other in (0, 1):
                got = value.at[step, half, 2 * way, pl.ds(0, side - 1 + other)]
                remote(
                    got, got, second_send.at[step, half, way], second_sem.at[step, half, way, other], sibling
                ).wait_recv()
        last = []
        for at in groups:
            total = value[step, half, at, 0]
            for slot in range(1, side):
                total = total + value[step, half, at, slot]
            last.append(total)
        last = jnp.concatenate(last, axis=1)
        solved[step, half * outs_half : (half + 1) * outs_half] = last
        return last

    load_right.wait()
    for at in range(all_loads):
        cut(1, at)
    later = []
    for step in range(steps):
        take_planes(step, 0)
        if step == 0:
            last_two = multiply_last(1)
            later = [
                multiply(1, range(5 * half, 5 * half + 4)) + last_two[half * outs_half : (half + 1) * outs_half]
                for half in range(HALVES)
            ]
        take_planes(step, 1)
        for half in range(HALVES):
            take_first(step, half)
        for half in range(HALVES):
            last = take_second(step, half)
            if step + 1 < steps:
                high, low = split(last)
                update = product(jnp.concatenate([high, low], axis=0), corner_split[...])
                update = update[:, 0:rows] + update[:, rows : 2 * rows]
                update = update[0:outs_half] + update[outs_half : 2 * outs_half]
                send_up(step + 1, half, later[half] + update)

    drain()


def local(side, planes, factor, inverses, right_side, earlier):
    steps, rows, _, width = factor.shape
    prior, share, outs = earlier.shape
    outs_half = outs // HALVES
    chunks = len(CHUNKS)
    dma, vmem = pltpu.SemaphoreType.DMA, pltpu.VMEM
    in_hbm = pl.BlockSpec(memory_space=pltpu.HBM)
    solved = pl.pallas_call(
        functools.partial(kernel, side, planes),
        name="falkon",
        out_shape=jax.ShapeDtypeStruct((steps, outs, width), F32),
        in_specs=[in_hbm] * 4,
        out_specs=pl.BlockSpec(memory_space=pltpu.VMEM),
        scratch_shapes=[
            *[vmem((CORES, side, side, len(units), 16, 128), F32) for chunk in CHUNKS for units in chunk],
            vmem((9, width, 256), BF16),
            vmem((steps, prior, rows, width), F32),
            vmem((steps, prior, 2 * rows, width), BF16),
            vmem((rows, width), F32),
            vmem((steps, width, rows), F32),
            vmem((steps, 2, 2 * rows, width), BF16),
            vmem((width, 2 * rows), BF16),
            vmem((steps, outs, rows), F32),
            vmem((prior, share, outs), F32),
            vmem((steps, HALVES, outs_half, rows), F32),
            vmem((steps, HALVES, planes - 1, outs_half, rows), F32),
            vmem((steps, HALVES, 2 * CORES, outs_half, 128), F32),
            vmem((steps, HALVES, 2, CORES * side, outs_half, 128), F32),
            vmem((steps, HALVES, 2 * CORES, side, outs_half, 128), F32),
            dma((16,)),
            dma((chunks,)),
            dma((chunks,)),
            dma((chunks,)),
            dma((chunks, 2, side)),
            dma((chunks, 2, side)),
            dma((chunks, 2, side)),
            dma((steps, HALVES)),
            dma((steps, HALVES)),
            dma((steps, HALVES, 2)),
            dma((steps, HALVES, 2)),
            dma((steps, HALVES, 2)),
            dma((steps, HALVES, 2, 2)),
            pltpu.SemaphoreType.REGULAR,
        ],
        compiler_params=pltpu.CompilerParams(
            collective_id=0, has_side_effects=True, vmem_limit_bytes=40 << 20
        ),
    )(
        *[
            pltpu.with_memory_space_constraint(array, pltpu.HBM)
            for array in (
                jnp.transpose(factor, (0, 2, 1, 3)),
                inverses,
                jnp.transpose(right_side, (0, 2, 1)),
                earlier,
            )
        ]
    )
    return jnp.transpose(solved, (0, 2, 1))


def solution(mesh):
    side = 1
    while side * side * CORES < mesh.shape["row"]:
        side += 1
    in_specs = (
        P(None, "row", None, "col"),
        P(None, "col", "row"),
        P(None, "row", None),
        P(None, ("col", "row"), None),
    )
    return jax.shard_map(
        functools.partial(local, side, mesh.shape["col"]),
        mesh=mesh,
        in_specs=in_specs,
        out_specs=P(None, "col", None),
        check_vma=False,
    )
```

```python
import functools

import jax
import jax.numpy as jnp
from jax import lax
from jax.experimental import pallas as pl
from jax.experimental.pallas import tpu as pltpu
from jax.sharding import PartitionSpec as P

MESH = pl.DeviceIdType.MESH
F32 = jnp.float32
BF16 = jnp.bfloat16
CORES = 2
HALVES = 2
CHUNKS = (((0, 1, 4), (2, 3)), ((5,), (7,)), ((6,), (8,)))


def split(value):
    high = value.astype(BF16)
    return high, (value - high.astype(F32)).astype(BF16)


def product(left, right):
    return jnp.dot(left, right, preferred_element_type=F32)


def kernel(
    side, planes, factor, inverses, right_side, earlier, solved,
    known_00, known_01, known_10, known_11, known_20, known_21, weights, tiles, tiles_split, corner, inverse, inverse_split, corner_split,
    right, early, mine, others, term, parts, value,
    load_sem, ring_send, group_send, core_send, ring_sem, group_sem, core_sem,
    z_send, z_sem, first_send, first_sem, second_send, second_sem, vouch_sem,
):
    known = ((known_00, known_01), (known_10, known_11), (known_20, known_21))
    steps, prior, rows, width = tiles.shape
    outs = right_side.shape[1]
    outs_half = outs // HALVES
    place = lax.axis_index("row")
    z = lax.axis_index("col")
    y, x, core = place // (side * CORES), (place // CORES) % side, place % CORES

    def device(dy, dx, other=0):
        to_core = core + other * (1 - 2 * core)
        return (((y + dy) % side * side + (x + dx) % side) * CORES + to_core, z)

    def above(dz):
        return (place, (z + dz) % planes)

    sibling = (place + 1 - 2 * core, z)
    far_ring = [2, 1, 3]
    near_first = [1, 3, 2]
    z_far_first = sorted(range(1, planes), key=lambda d: -min(d, planes - d))

    copies = []

    def load(source, target):
        copy = pltpu.make_async_copy(source, target, load_sem.at[len(copies)])
        copy.start()
        copies.append(copy)
        return copy

    load_early = load(earlier, early)

    greeted = [device(d * turn, d * (1 - turn)) for d in far_ring for turn in (0, 1)]
    greeted += [above(dz) for dz in (2, planes - 2, 1, planes - 1)] + [sibling]
    barrier = pltpu.get_barrier_semaphore()
    for to in greeted:
        pl.semaphore_signal(barrier, inc=1, device_id=to, device_id_type=MESH)

    group = 3
    load_tiles = [[], []]

    def load_step(step):
        for at in range(prior // group):
            blocks = pl.ds(at * group, group)
            load_tiles[step].append(load(factor.at[step, blocks], tiles.at[step, blocks]))

    load_step(0)
    load_right = load(right_side, right)
    load_inverse = load(inverses, inverse)
    load_corner = load(factor.at[1, prior], corner)
    load_step(1)

    turns = [(part + core) % 2 for part in range(2)]
    outer = [y * (1 - turn) + x * turn for turn in turns]
    inner = [x * (1 - turn) + y * turn for turn in turns]
    load_early.wait()
    def pack(chunk):
        for part, units in enumerate(CHUNKS[chunk]):
            for at, unit in enumerate(units):
                if unit == 4:
                    pieces = [early[16], early[17]]
                else:
                    first = 4 * (unit % 5)
                    columns = slice(0, outs_half) if unit < 4 else slice(outs_half, outs)
                    pieces = [early[first + block, :, columns] for block in range(4)]
                known[chunk][part][core, outer[part], inner[part], at] = jnp.concatenate(pieces, axis=1)

    pack(0)
    pl.semaphore_wait(barrier, len(greeted))
    vouched_by = [above(2), above(planes - 2), sibling]
    for to in vouched_by:
        pl.semaphore_signal(vouch_sem, inc=1, device_id=to, device_id_type=MESH)

    def ring(part, distance):
        return device(distance * turns[part], distance * (1 - turns[part]))

    def across(part, distance):
        return device(distance * (1 - turns[part]), distance * turns[part])

    def remote(source, target, send, recv, to):
        return pltpu.make_async_remote_copy(
            src_ref=source, dst_ref=target, send_sem=send, recv_sem=recv, device_id=to, device_id_type=MESH
        )

    def piece(chunk, part, distance):
        return known[chunk][part].at[core, outer[part], (inner[part] + distance) % side]

    def whole(chunk, part, distance):
        return known[chunk][part].at[core, (outer[part] + distance) % side]

    def whole_other(chunk, part, distance):
        return known[chunk][part].at[1 - core, (inner[part] + distance) % side]

    def go_round(chunk, part, distance):
        own = piece(chunk, part, 0)
        return remote(own, own, ring_send.at[chunk], ring_sem.at[chunk, part, distance], ring(part, distance))

    def go_across(chunk, part, held, distance):
        own = piece(chunk, part, held)
        return remote(own, own, group_send.at[chunk], group_sem.at[chunk, part, distance], across(part, distance))

    def go_over(chunk, part, distance):
        own = whole(chunk, part, distance)
        return remote(own, own, core_send.at[chunk], core_sem.at[chunk, part, distance], sibling)

    chunks = range(len(CHUNKS))

    def drain():
        for chunk in chunks:
            for part in range(2):
                for sent, got in (
                    (ring_send, known[chunk][part].at[0, 0, pl.ds(0, side - 1)]),
                    (group_send, known[chunk][part].at[0, pl.ds(0, side - 1)]),
                    (core_send, known[chunk][part].at[0]),
                ):
                    remote(got, got, sent.at[chunk], ring_sem.at[0, 0, 0], sibling).wait_send()
        for step in range(steps):
            for half in range(HALVES):
                got = others.at[step, half]
                remote(got, got, z_send.at[step, half], z_sem.at[step, half], sibling).wait_send()
                for way in range(2):
                    got = parts.at[step, half, way, pl.ds(0, CORES * side - 1)]
                    remote(got, got, first_send.at[step, half, way], z_sem.at[step, half], sibling).wait_send()
                    remote(got, got, second_send.at[step, half, way], z_sem.at[step, half], sibling).wait_send()

    def ring_out(chunk):
        for distance in far_ring:
            for part in range(2):
                go_round(chunk, part, distance).start()

    def across_out(chunk):
        for distance in far_ring:
            for part in range(2):
                go_across(chunk, part, 0, distance).start()

    def cut(step, at):
        load_tiles[step][at].wait()

        def one(block, carry):
            high, low = split(tiles[step, block])
            tiles_split[step, block, 0:rows] = high
            tiles_split[step, block, rows : 2 * rows] = low
            return carry

        lax.fori_loop(at * group, (at + 1) * group, one, 0)

    lane = lax.broadcasted_iota(jnp.int32, (rows, 128), 1)

    def unpack(chunk, part, distance, other):
        at_outer = ((inner if other else outer)[part] + distance) % side
        turn = 1 - turns[part] if other else turns[part]
        at_core = 1 - core if other else core
        for at_inner in range(side):
            at_y, at_x = at_outer * (1 - turn) + at_inner * turn, at_inner * (1 - turn) + at_outer * turn
            row = pl.multiple_of(((at_y * side + at_x) * CORES + at_core) * 16, 16)
            for at, unit in enumerate(CHUNKS[chunk][part]):
                high, low = split(known[chunk][part][at_core, at_outer, at_inner, at])
                weights[unit, pl.ds(row, 16), 0:128] = high
                weights[unit, pl.ds(row, 16), 128:256] = low

    def ring_in(chunk):
        for distance in near_first:
            for part in range(2):
                go_round(chunk, part, distance).wait_recv()
                for onward in far_ring:
                    go_across(chunk, part, side - distance, onward).start()
        for part in range(2):
            go_over(chunk, part, 0).start()

    def across_in(chunk, distances=(0, *near_first)):
        for distance in distances:
            for part in range(2):
                if distance > 0:
                    got = whole(chunk, part, side - distance)
                    remote(got, got, group_send.at[chunk], group_sem.at[chunk, part, distance], sibling).wait_recv()
                    go_over(chunk, part, side - distance).start()
                unpack(chunk, part, (side - distance) % side, False)

    def over_in(chunk):
        for distance in [0] + near_first:
            for part in range(2):
                got = whole_other(chunk, part, distance)
                remote(got, got, core_send.at[chunk], core_sem.at[chunk, part, distance], sibling).wait_recv()
                unpack(chunk, part, distance, True)

    def multiply(step, units):
        total = None
        for unit in units:
            first = 4 * (unit % 5)
            left = tiles_split[step, first : first + 4].reshape(4 * 2 * rows, width)
            term_of = product(left, weights[unit])
            total = term_of if total is None else total + term_of
        found = None
        for block in reversed(range(4)):
            at = 2 * rows * block
            both = total[at : at + rows] + total[at + rows : at + 2 * rows]
            both = both[:, 0:128] + both[:, 128:256]
            found = both if found is None else jnp.where(lane < outs_half * (block + 1), both, found)
        turned = jnp.transpose(found)
        return (turned[0:32] + turned[32:64]) + (turned[64:96] + turned[96:128])

    def multiply_last(step):
        total = product(tiles_split[step, 16:18].reshape(2 * 2 * rows, width), weights[4])
        found = None
        for block in reversed(range(2)):
            at = 2 * rows * block
            both = total[at : at + rows] + total[at + rows : at + 2 * rows]
            both = both[:, 0:128] + both[:, 128:256]
            found = both if found is None else jnp.where(lane < outs, both, found)
        turned = jnp.transpose(found)
        return turned[0:outs] + turned[outs : 2 * outs]

    def send_up(step, half, part_sum):
        mine[step, half] = part_sum
        for dz in z_far_first:
            remote(
                mine.at[step, half], others.at[step, half, dz - 1], z_send.at[step, half], z_sem.at[step, half], above(dz)
            ).start()

    def prepare():
        load_inverse.wait()
        for step in range(steps):
            high, low = split(jnp.transpose(inverse[step]))
            inverse_split[step, 0, 0:rows] = high
            inverse_split[step, 0, rows : 2 * rows] = high
            inverse_split[step, 1, 0:rows] = low
            inverse_split[step, 1, rows : 2 * rows] = low
        load_corner.wait()
        high, low = split(jnp.transpose(corner[...]))
        corner_split[:, 0:rows] = high
        corner_split[:, rows : 2 * rows] = low

    all_loads = prior // group
    ring_out(0)
    across_out(0)
    for chunk in chunks[1:]:
        pack(chunk)
    ring_out(1)
    ring_out(2)
    cut(0, 0)
    cut(0, 1)
    ring_in(0)
    across_out(1)
    cut(0, 2)
    cut(0, 3)
    cut(0, 4)
    cut(0, 5)
    prepare()
    ring_in(1)
    across_in(0, (0, 1))
    across_out(2)
    ring_in(2)
    across_in(0, (3, 2))
    over_in(0)
    pl.semaphore_wait(vouch_sem, len(vouched_by))
    last_two = multiply_last(0)
    send_up(0, 0, multiply(0, (0, 1, 2, 3)) + last_two[0:outs_half])
    across_in(1)
    across_in(2)
    over_in(1)
    partial = multiply(0, (5, 7)) + last_two[outs_half:outs]
    over_in(2)
    send_up(0, 1, partial + multiply(0, (6, 8)))

    coordinates = (x, y)
    in_plane = ((2, 1), (2, 0), (1, 1), (3, 1), (1, 0), (3, 0), (0, 1))
    groups = range(width // 128)

    def along(way, distance, other):
        return device(distance * way, distance * (1 - way), other)

    def take_planes(step, half):
        got = others.at[step, half]
        remote(got, got, z_send.at[step, half], z_sem.at[step, half], sibling).wait_recv()
        total = mine[step, half]
        for dz in range(planes - 1):
            total = total + others[step, half, dz]
        high, low = split(right[step, half * outs_half : (half + 1) * outs_half] - total)
        both = jnp.concatenate([high, low], axis=1)
        result = product(both, inverse_split[step, 0]) + product(both, inverse_split[step, 1])
        for at in groups:
            term[step, half, at] = result[:, 128 * at : 128 * at + 128]
        for way in range(2):
            slot = CORES * coordinates[way] + core
            parts[step, half, way, slot] = term[step, half, 2 * way + core]
            for distance, other in in_plane:
                remote(
                    term.at[step, half, 2 * way + core + other * (1 - 2 * core)], parts.at[step, half, way, slot],
                    first_send.at[step, half, way], first_sem.at[step, half, way], along(way, distance, other),
                ).start()

    def take_first(step, half):
        for way in range(2):
            got = parts.at[step, half, way, pl.ds(0, CORES * side - 1)]
            remote(got, got, first_send.at[step, half, way], first_sem.at[step, half, way], sibling).wait_recv()
            total = parts[step, half, way, 0]
            for slot in range(1, CORES * side):
                total = total + parts[step, half, way, slot]
            slot = coordinates[1 - way]
            value[step, half, 2 * way + core, slot] = total
            own = value.at[step, half, 2 * way + core, slot]
            for distance, other in in_plane:
                remote(
                    own, own, second_send.at[step, half, way], second_sem.at[step, half, way, other],
                    along(1 - way, distance, other),
                ).start()

    def take_second(step, half):
        for way in range(2):
            for other in (0, 1):
                got = value.at[step, half, 2 * way, pl.ds(0, side - 1 + other)]
                remote(
                    got, got, second_send.at[step, half, way], second_sem.at[step, half, way, other], sibling
                ).wait_recv()
        last = []
        for at in groups:
            total = value[step, half, at, 0]
            for slot in range(1, side):
                total = total + value[step, half, at, slot]
            last.append(total)
        last = jnp.concatenate(last, axis=1)
        solved[step, half * outs_half : (half + 1) * outs_half] = last
        return last

    load_right.wait()
    for at in range(all_loads):
        cut(1, at)
    later = []
    for step in range(steps):
        take_planes(step, 0)
        if step == 0:
            last_two = multiply_last(1)
            later = [
                multiply(1, range(5 * half, 5 * half + 4)) + last_two[half * outs_half : (half + 1) * outs_half]
                for half in range(HALVES)
            ]
        take_planes(step, 1)
        for half in range(HALVES):
            take_first(step, half)
        for half in range(HALVES):
            last = take_second(step, half)
            if step + 1 < steps:
                high, low = split(last)
                update = product(jnp.concatenate([high, low], axis=0), corner_split[...])
                update = update[:, 0:rows] + update[:, rows : 2 * rows]
                update = update[0:outs_half] + update[outs_half : 2 * outs_half]
                send_up(step + 1, half, later[half] + update)

    drain()


def local(side, planes, factor, inverses, right_side, earlier):
    steps, rows, _, width = factor.shape
    prior, share, outs = earlier.shape
    outs_half = outs // HALVES
    chunks = len(CHUNKS)
    dma, vmem = pltpu.SemaphoreType.DMA, pltpu.VMEM
    in_hbm = pl.BlockSpec(memory_space=pltpu.HBM)
    solved = pl.pallas_call(
        functools.partial(kernel, side, planes),
        name="falkon",
        out_shape=jax.ShapeDtypeStruct((steps, outs, width), F32),
        in_specs=[in_hbm] * 4,
        out_specs=pl.BlockSpec(memory_space=pltpu.VMEM),
        scratch_shapes=[
            *[vmem((CORES, side, side, len(units), 16, 128), F32) for chunk in CHUNKS for units in chunk],
            vmem((9, width, 256), BF16),
            vmem((steps, prior, rows, width), F32),
            vmem((steps, prior, 2 * rows, width), BF16),
            vmem((rows, width), F32),
            vmem((steps, width, rows), F32),
            vmem((steps, 2, 2 * rows, width), BF16),
            vmem((width, 2 * rows), BF16),
            vmem((steps, outs, rows), F32),
            vmem((prior, share, outs), F32),
            vmem((steps, HALVES, outs_half, rows), F32),
            vmem((steps, HALVES, planes - 1, outs_half, rows), F32),
            vmem((steps, HALVES, 2 * CORES, outs_half, 128), F32),
            vmem((steps, HALVES, 2, CORES * side, outs_half, 128), F32),
            vmem((steps, HALVES, 2 * CORES, side, outs_half, 128), F32),
            dma((16,)),
            dma((chunks,)),
            dma((chunks,)),
            dma((chunks,)),
            dma((chunks, 2, side)),
            dma((chunks, 2, side)),
            dma((chunks, 2, side)),
            dma((steps, HALVES)),
            dma((steps, HALVES)),
            dma((steps, HALVES, 2)),
            dma((steps, HALVES, 2)),
            dma((steps, HALVES, 2)),
            dma((steps, HALVES, 2, 2)),
            pltpu.SemaphoreType.REGULAR,
        ],
        compiler_params=pltpu.CompilerParams(
            collective_id=0, has_side_effects=True, vmem_limit_bytes=40 << 20
        ),
    )(
        *[
            pltpu.with_memory_space_constraint(array, pltpu.HBM)
            for array in (
                jnp.transpose(factor, (0, 2, 1, 3)),
                inverses,
                jnp.transpose(right_side, (0, 2, 1)),
                earlier,
            )
        ]
    )
    return jnp.transpose(solved, (0, 2, 1))


def solution(mesh):
    side = 1
    while side * side * CORES < mesh.shape["row"]:
        side += 1
    in_specs = (
        P(None, "row", None, "col"),
        P(None, "col", "row"),
        P(None, "row", None),
        P(None, ("col", "row"), None),
    )
    return jax.shard_map(
        functools.partial(local, side, mesh.shape["col"]),
        mesh=mesh,
        in_specs=in_specs,
        out_specs=P(None, "col", None),
        check_vma=False,
    )
```
